256 devices in a mesh: ctx: 128 (over z, x_hi, y, core), tp: 2 (over x_lo).
Axes of the slice: x: 4 (x_hi: 2, x_lo: 2; x = x_hi * 2 + x_lo), y: 4, z: 8, core: 2. Of those that a mesh axis runs over, the one named last changes fastest.
Arguments:
- queries: bfloat16 [8192, 1536], P('ctx', 'tp'), may hold values from -512 to 512
- keys: bfloat16 [8192, 1536], P('ctx', 'tp'), may hold values from -8 to 8
- values: bfloat16 [8192, 1536], P('ctx', 'tp'), may hold values from -6 to 6
- wo: bfloat16 [1536, 3072], P('tp'), may hold values from -0.15625 to 0.15625
- frame_tokens: int32 [128], replicated, may hold values from 32 to 64, as said below
Outputs:
- projected: bfloat16 [8192, 3072], P(('ctx', 'tp'))
The draws below stay inside these ranges and needn't reach their ends.
Inputs may be any that keep to these rules, and one draw needn't show every extreme that they name: `frame_tokens`: at least 32 tokens of every frame are live.
All inputs are finite; a program needn't handle non-finite values.
Results may differ from the reference program's by a relative error of at most 0.014.
Values may be sent and summed in bfloat16 or wider, within the bound.
No kernel may reach another device: no remote copies, remote signals or barrier semaphores. Data moves between devices by JAX's collectives and lax.ppermute only.
A program may use at most 128 MiB of HBM per device.

```python
import math
import jax
import jax.numpy as jnp
from jax import lax

WIDTH = 3072
HEADS = 12
HEAD_DIM = 128
FRAME = 64
FRAMES = 128
TOKENS = 8192


def shared_fields(key):
    columns = HEADS * HEAD_DIM
    key_drawn = jnp.clip(jax.random.normal(jax.random.fold_in(key, 11), (TOKENS, columns), jnp.float32), -6.0, 6.0)
    query_drawn = jnp.clip(2.5 * jax.random.normal(jax.random.fold_in(key, 12), (TOKENS, columns), jnp.float32), -15.0, 15.0)
    return (key_drawn, query_drawn)


def draw_queries(key, part):
    key_field, query_field = shared_fields(key)
    return query_field.astype(jnp.bfloat16)


def draw_keys(key, part):
    key_field, query_field = shared_fields(key)
    return key_field.astype(jnp.bfloat16)


def draw_frame_tokens(key, part):
    counts = jax.random.randint(jax.random.fold_in(key, 21), (FRAMES,), FRAME // 2, FRAME + 1)
    fullest = jax.random.randint(jax.random.fold_in(key, 22), (), 0, FRAMES)
    emptiest = jax.random.randint(jax.random.fold_in(key, 23), (), 0, FRAMES)
    frame_ids = jnp.arange(FRAMES, dtype=jnp.int32)
    counts = jnp.where(frame_ids == emptiest, FRAME // 2, counts)
    counts = jnp.where(frame_ids == fullest, FRAME, counts)
    return counts.astype(jnp.int32)


def shard_levels(own_key, dims, cuts, smallest, high):
    level, own = 1.0, jax.random.fold_in(own_key, 6)
    for dim, shards_of in cuts:
        steps = jnp.exp(jax.random.uniform(jax.random.fold_in(own, dim), (shards_of,), jnp.float32, smallest / len(cuts), high / len(cuts)))
        level = level * jnp.repeat(steps, dims[dim] // shards_of).reshape([-1 if axis == dim else 1 for axis in range(len(dims))])
    return level


def normal_values(rng, extent, deviation, bound, cuts=(), kind=jnp.bfloat16):
    gain = shard_levels(rng, extent, cuts, -0.22, 0.18) if cuts else 1.0
    values = jax.random.normal(rng, extent, jnp.float32) * deviation * gain
    return jnp.minimum(jnp.maximum(values, -bound), bound).astype(kind)


def setup_inputs(seed: int = 0) -> dict:
    arg_keys = jax.random.split(jax.random.key(seed), 6)
    queries = draw_queries(jax.random.fold_in(arg_keys[5], 71), 0)
    keys = draw_keys(jax.random.fold_in(arg_keys[5], 71), 0)
    values = normal_values(arg_keys[2], (TOKENS, HEADS * HEAD_DIM), 1.0, 6.0, ((0, 128), (1, 2)))
    wo = normal_values(arg_keys[3], (HEADS * HEAD_DIM, WIDTH), (HEADS * HEAD_DIM) ** -0.5, 0.15625, ((0, 2),))
    frame_tokens = draw_frame_tokens(jax.random.fold_in(arg_keys[5], 71), 0)
    return {"queries": queries, "keys": keys, "values": values, "wo": wo, "frame_tokens": frame_tokens}


def reference(queries, keys, values, wo, frame_tokens):
    total_rows = queries.shape[0]
    positions = jnp.arange(total_rows, dtype=jnp.int32)
    frame_index = positions // FRAME
    live_mask = positions % FRAME < frame_tokens[frame_index]
    query_all = queries.astype(jnp.float32).reshape(total_rows, HEADS, HEAD_DIM)
    key_all = keys.astype(jnp.float32).reshape(total_rows, HEADS, HEAD_DIM)
    value_all = values.astype(jnp.float32).reshape(total_rows, HEADS, HEAD_DIM)
    block_rows = 512 if total_rows % 512 == 0 else total_rows
    scale_factor = 1.0 / math.sqrt(HEAD_DIM)

    def one_block(start):
        query_block = lax.dynamic_slice_in_dim(query_all, start, block_rows, 0)
        frame_block = lax.dynamic_slice_in_dim(frame_index, start, block_rows, 0)
        live_block = lax.dynamic_slice_in_dim(live_mask, start, block_rows, 0)
        scores = jnp.einsum('qhd,khd->hqk', query_block, key_all) * scale_factor
        allowed = (frame_index[None, :] <= frame_block[:, None]) & live_mask[None, :]
        scores = jnp.where(allowed[None], scores, -jnp.inf)
        row_max = lax.optimization_barrier(jnp.max(scores, axis=-1, keepdims=True))
        weights = jnp.exp(scores - row_max)
        totals = lax.optimization_barrier(jnp.sum(weights, axis=-1))
        rounded = lax.optimization_barrier(weights.astype(jnp.bfloat16)).astype(jnp.float32)
        summed = jnp.einsum('hqk,khd->qhd', rounded, value_all)
        heads_out = summed / jnp.transpose(totals)[:, :, None]
        heads_out = jnp.where(live_block[:, None, None], heads_out, 0.0)
        return heads_out.astype(jnp.bfloat16)
    block_starts = jnp.arange(0, total_rows, block_rows, dtype=jnp.int32)
    blocks_out = lax.map(one_block, block_starts)
    attended = blocks_out.reshape(total_rows, HEADS * HEAD_DIM)
    return jnp.dot(attended, wo, preferred_element_type=jnp.float32).astype(jnp.bfloat16)
```

```python
import functools
import math

import jax
import jax.numpy as jnp
from jax import lax
from jax.experimental import pallas as pl
from jax.experimental.pallas import tpu as pltpu
from jax.sharding import Mesh, PartitionSpec as P

HEAD_DIM = 128
FRAME = 64
PLANES = 8
COLUMNS = 8
HEADS = 6
WIDE = HEADS * HEAD_DIM
STATS = 128
CTX = ("z", "xh", "y", "core")
MASKED = -(2.0**24)
FLOOR = -(2.0**22)
EXP2_SCALE = math.log2(math.e) / math.sqrt(HEAD_DIM)


def fill_bias(bias_ref, frames, counts_ref, my_plane, my_core):
    rows = lax.broadcasted_iota(jnp.int32, (FRAME, 128), 0)
    lanes = lax.broadcasted_iota(jnp.int32, (FRAME, 128), 1)
    query_frames = (my_plane * COLUMNS + lanes) * 2 + my_core
    for i, frame in enumerate(frames):
        allowed = (rows < counts_ref[frame]) & (frame <= query_frames)
        bias_ref[i * FRAME : (i + 1) * FRAME, :] = jnp.where(allowed, 0.0, MASKED).astype(
            jnp.bfloat16
        )


def block_frame(place, offset, other):
    plane, column, core = place
    block_plane = lax.rem(plane + offset + PLANES, PLANES)
    return (block_plane * COLUMNS + column) * 2 + (1 - core if other else core)


def attend(offsets, has_state, last, *refs):
    place_ref, counts_ref, q_ref, *refs = refs
    kv_refs, refs = refs[: len(offsets)], refs[len(offsets) :]
    if has_state:
        acc_in, max_in, sum_in, *refs = refs
    outs, (bias_ref, hot_ref) = refs[:-2], refs[-2:]
    place = plane, column, core = place_ref[0], place_ref[1], place_ref[2]
    sign = 2 * core - 1
    blocks, frames = [], []
    for ref, (kind, distance, other_sender) in zip(kv_refs, offsets):
        direction = -sign if other_sender else sign
        for slot in range(2):
            if kind == "half":
                break
            blocks.append((ref, slot))
            frames.append(block_frame(place, direction * distance, (slot == 1) != other_sender))
        if kind == "half":
            blocks.append((ref, 0))
            frames.append(block_frame(place, distance, other_sender))
    fill_bias(bias_ref, frames, counts_ref, plane, core)
    rows = lax.broadcasted_iota(jnp.int32, (FRAME, 128), 1)
    for j in range(COLUMNS):
        hot_ref[j * FRAME : (j + 1) * FRAME, :] = jnp.where(rows == j, 1.0, 0.0).astype(jnp.bfloat16)
    keys_n = len(blocks) * FRAME
    ones = jnp.ones((keys_n, 128), jnp.bfloat16)
    q_tile = 256
    for h in range(HEADS):
        cols = slice(h * HEAD_DIM, (h + 1) * HEAD_DIM)
        k_head = jnp.concatenate([ref[slot, 0, :, cols] for ref, slot in blocks], axis=0)
        v_head = jnp.concatenate([ref[slot, 1, :, cols] for ref, slot in blocks], axis=0)
        k_wide = jnp.concatenate([k_head, bias_ref[...]], axis=1)
        v_wide = jnp.concatenate([v_head, ones], axis=1)
        for t in range(COLUMNS * FRAME // q_tile):
            at = slice(t * q_tile, (t + 1) * q_tile)
            frames_at = slice(t * q_tile // FRAME, (t + 1) * q_tile // FRAME)
            q_head = q_ref[frames_at, :, cols].reshape(q_tile, HEAD_DIM)
            q_wide = jnp.concatenate([q_head, hot_ref[at, :]], axis=1)
            scores = lax.dot_general(
                q_wide, k_wide, (((1,), (1,)), ((), ())), preferred_element_type=jnp.float32
            )
            top = jnp.maximum(jnp.max(scores, axis=1, keepdims=True), FLOOR)
            if has_state:
                before = max_in[at, h : h + 1]
                top = jnp.maximum(top, before)
            weights = jnp.exp2((scores - top) * EXP2_SCALE).astype(jnp.bfloat16)
            both = jnp.dot(weights, v_wide, preferred_element_type=jnp.float32)
            acc, total = both[:, :HEAD_DIM], both[:, HEAD_DIM : HEAD_DIM + 1]
            if has_state:
                fade = jnp.exp2((before - top) * EXP2_SCALE)
                acc = acc + acc_in[at, cols] * fade
                total = total + sum_in[at, h : h + 1] * fade
            if not last:
                acc_out, max_out, sum_out = outs
                acc_out[at, cols] = acc
                max_out[at, h : h + 1] = top
                sum_out[at, h : h + 1] = total
            else:
                (out,) = outs
                mean = (acc * (1.0 / jnp.maximum(total, 1e-30))).astype(jnp.bfloat16)
                out[frames_at, :, cols] = mean.reshape(q_tile // FRAME, FRAME, HEAD_DIM)
                parts = []
                for value, count in ((top, 3), (total, 2)):
                    for _ in range(count):
                        part = value.astype(jnp.bfloat16)
                        parts.append(part)
                        value = value - part.astype(jnp.float32)
                for i, part in enumerate(parts):
                    lane = WIDE + h * 8 + i
                    out[frames_at, :, lane : lane + 1] = part.reshape(q_tile // FRAME, FRAME, 1)


def attend_call(place, counts, q_all, kv, offsets, state, last):
    rows = COLUMNS * FRAME
    keys_n = sum(1 if kind == "half" else 2 for kind, _, _ in offsets) * FRAME
    if last:
        out_shape = jax.ShapeDtypeStruct((COLUMNS, FRAME, WIDE + STATS), jnp.bfloat16)
        out_specs = pl.BlockSpec(memory_space=pltpu.VMEM)
    else:
        out_shape = [
            jax.ShapeDtypeStruct((rows, WIDE), jnp.float32),
            jax.ShapeDtypeStruct((rows, 128), jnp.float32),
            jax.ShapeDtypeStruct((rows, 128), jnp.float32),
        ]
        out_specs = [pl.BlockSpec(memory_space=pltpu.VMEM)] * 3
    vmem = pl.BlockSpec(memory_space=pltpu.VMEM)
    smem = pl.BlockSpec(memory_space=pltpu.SMEM)
    flops = 2 * 2 * rows * keys_n * WIDE
    return pl.pallas_call(
        functools.partial(attend, offsets, state is not None, last),
        out_shape=out_shape,
        in_specs=[smem, smem] + [vmem] * (1 + len(kv) + (3 if state is not None else 0)),
        out_specs=out_specs,
        scratch_shapes=[
            pltpu.VMEM((keys_n, 128), jnp.bfloat16),
            pltpu.VMEM((rows, 128), jnp.bfloat16),
        ],
        compiler_params=pltpu.CompilerParams(vmem_limit_bytes=40 * 2**20),
        cost_estimate=pl.CostEstimate(
            flops=flops, bytes_accessed=4 * 2**20, transcendentals=rows * keys_n * HEADS
        ),
        name="attend_last" if last else "attend_first",
    )(place, counts, q_all, *kv, *(state if state is not None else ()))


def project(tp_count, place_ref, counts_ref, parts_ref, wo_ref, send_ref, keep_ref, att_ref):
    plane, column, core, tp = place_ref[0], place_ref[1], place_ref[2], place_ref[3]
    frame = (plane * COLUMNS + column) * 2 + core
    rows = lax.broadcasted_iota(jnp.int32, (FRAME, 1), 0)
    live = rows < counts_ref[frame]
    for h in range(HEADS):
        cols = slice(h * HEAD_DIM, (h + 1) * HEAD_DIM)
        tops, totals = [], []
        for j in range(COLUMNS):
            lane = WIDE + h * 8
            st = parts_ref[j, :, WIDE : WIDE + STATS].astype(jnp.float32)
            st = st[:, h * 8 : h * 8 + 5]
            tops.append(st[:, 0:1] + st[:, 1:2] + st[:, 2:3])
            totals.append(st[:, 3:4] + st[:, 4:5])
        top = functools.reduce(jnp.maximum, tops)
        shares = [n * jnp.exp2((m - top) * EXP2_SCALE) for m, n in zip(tops, totals)]
        total = functools.reduce(jnp.add, shares)
        acc = functools.reduce(
            jnp.add,
            [parts_ref[j, :, cols].astype(jnp.float32) * shares[j] for j in range(COLUMNS)],
        )
        out = jnp.where(live, acc / total, 0.0)
        att_ref[:, cols] = out.astype(jnp.bfloat16)
    half = FRAME // tp_count
    mine = pl.ds(pl.multiple_of(tp * half, half), half)
    theirs = pl.ds(pl.multiple_of((1 - tp) * half, half), half)
    att = jnp.concatenate([att_ref[theirs, :], att_ref[mine, :]], axis=0)
    step = 512
    for n in range(0, wo_ref.shape[1], step):
        out = jnp.dot(att, wo_ref[:, n : n + step], preferred_element_type=jnp.float32)
        send_ref[:, n : n + step] = out[:half].astype(jnp.bfloat16)
        keep_ref[:, n : n + step] = out[half:]


def project_call(place, counts, parts, wo):
    vmem = pl.BlockSpec(memory_space=pltpu.VMEM)
    smem = pl.BlockSpec(memory_space=pltpu.SMEM)
    width = wo.shape[1]
    return pl.pallas_call(
        functools.partial(project, 2),
        out_shape=[
            jax.ShapeDtypeStruct((FRAME // 2, width), jnp.bfloat16),
            jax.ShapeDtypeStruct((FRAME // 2, width), jnp.float32),
        ],
        in_specs=[smem, smem, vmem, vmem],
        out_specs=[vmem, vmem],
        scratch_shapes=[pltpu.VMEM((FRAME, WIDE), jnp.bfloat16)],
        compiler_params=pltpu.CompilerParams(vmem_limit_bytes=40 * 2**20),
        name="project",
    )(place, counts, parts, wo)


SWAP = [(0, 1), (1, 0)]


def split_ring(distance):
    return [
        (z * 2 + c, (z + (distance if c == 0 else -distance)) % PLANES * 2 + c)
        for z in range(PLANES)
        for c in range(2)
    ]


def on_device(queries, keys, values, wo, frame_tokens):
    place = jnp.stack(
        [
            lax.axis_index("z"),
            lax.axis_index("xh") * 4 + lax.axis_index("y"),
            lax.axis_index("core"),
            lax.axis_index("tp"),
        ]
    ).astype(jnp.int32)
    own = jnp.stack([keys, values])
    own2 = jnp.stack([own, lax.ppermute(own, "core", SWAP)])
    zc = ("z", "core")
    near = lax.ppermute(own2, zc, split_ring(1))
    second = lax.ppermute(own2, zc, split_ring(2))
    q_all = lax.all_to_all(
        jnp.broadcast_to(queries[None], (COLUMNS, FRAME, WIDE)), ("xh", "y"), 0, 0, tiled=True
    )
    third = lax.ppermute(second, zc, split_ring(1))
    fourth = lax.ppermute(second[:1], zc, split_ring(2))
    near_o = lax.ppermute(near, "core", SWAP)
    second_o = lax.ppermute(second, "core", SWAP)
    third_o = lax.ppermute(third, "core", SWAP)
    fourth_o = lax.ppermute(fourth, "core", SWAP)
    first = [own2, near, near_o, second, second_o]
    first_off = [
        ("both", 0, False),
        ("both", 1, False),
        ("both", 1, True),
        ("both", 2, False),
        ("both", 2, True),
    ]
    rest = [third, third_o, fourth, fourth_o]
    rest_off = [("both", 3, False), ("both", 3, True), ("half", 4, False), ("half", 4, True)]
    state = attend_call(place, frame_tokens, q_all, first, first_off, None, False)
    partial = attend_call(place, frame_tokens, q_all, rest, rest_off, state, True)
    parts = lax.all_to_all(partial, ("xh", "y"), 0, 0, tiled=True)
    send, keep = project_call(place, frame_tokens, parts, wo)
    got = lax.ppermute(send, "tp", SWAP)
    return (keep + got.astype(jnp.float32)).astype(jnp.bfloat16)


def solution(mesh):
    fine = Mesh(mesh.devices.reshape(PLANES, 2, 4, 2, 2), CTX + ("tp",))
    in_specs = (P(CTX, "tp"), P(CTX, "tp"), P(CTX, "tp"), P("tp", None), P())
    out_specs = P(CTX + ("tp",), None)
    return jax.shard_map(
        on_device, mesh=fine, in_specs=in_specs, out_specs=out_specs, check_vma=False
    )
```

```python
import functools
import math

import jax
import jax.numpy as jnp
from jax import lax
from jax.experimental import pallas as pl
from jax.experimental.pallas import tpu as pltpu
from jax.sharding import Mesh, PartitionSpec as P

HEAD_DIM = 128
FRAME = 64
PLANES = 8
COLUMNS = 8
HEADS = 6
WIDE = HEADS * HEAD_DIM
STATS = 128
TOP_PARTS, TOTAL_PARTS = 3, 2
Q_TILE = 256
CTX = ("z", "xh", "y", "core")
MASKED = -(2.0**24)
FLOOR = -(2.0**22)
EXP2_SCALE = math.log2(math.e) / math.sqrt(HEAD_DIM)


def fill_bias(bias_ref, frames, counts_ref, my_plane, my_core):
    rows = lax.broadcasted_iota(jnp.int32, (FRAME, 128), 0)
    lanes = lax.broadcasted_iota(jnp.int32, (FRAME, 128), 1)
    query_frames = (my_plane * COLUMNS + lanes) * 2 + my_core
    for i, frame in enumerate(frames):
        allowed = (rows < counts_ref[frame]) & (frame <= query_frames)
        bias_ref[i * FRAME : (i + 1) * FRAME, :] = jnp.where(allowed, 0.0, MASKED).astype(
            jnp.bfloat16
        )


def block_frame(place, offset, other):
    plane, column, core = place
    block_plane = lax.rem(plane + offset + PLANES, PLANES)
    return (block_plane * COLUMNS + column) * 2 + (1 - core if other else core)


def attend(offsets, has_state, last, *refs):
    place_ref, counts_ref, q_ref, *refs = refs
    kv_refs, refs = refs[: len(offsets)], refs[len(offsets) :]
    if has_state:
        acc_in, max_in, sum_in, *refs = refs
    outs, (bias_ref, hot_ref) = refs[:-2], refs[-2:]
    place = plane, column, core = place_ref[0], place_ref[1], place_ref[2]
    sign = 2 * core - 1
    blocks, frames = [], []
    for ref, (kind, distance, other_sender) in zip(kv_refs, offsets):
        direction = -sign if other_sender else sign
        for slot in range(2):
            if kind == "half":
                break
            blocks.append((ref, slot))
            frames.append(block_frame(place, direction * distance, (slot == 1) != other_sender))
        if kind == "half":
            blocks.append((ref, 0))
            frames.append(block_frame(place, distance, other_sender))
    fill_bias(bias_ref, frames, counts_ref, plane, core)
    rows = lax.broadcasted_iota(jnp.int32, (FRAME, 128), 1)
    for j in range(COLUMNS):
        hot_ref[j * FRAME : (j + 1) * FRAME, :] = jnp.where(rows == j, 1.0, 0.0).astype(jnp.bfloat16)
    keys_n = len(blocks) * FRAME
    ones = jnp.ones((keys_n, 128), jnp.bfloat16)
    lanes = lax.broadcasted_iota(jnp.int32, (Q_TILE, 128), 1)
    for t in range(COLUMNS * FRAME // Q_TILE):
        at = slice(t * Q_TILE, (t + 1) * Q_TILE)
        frames_at = slice(t * Q_TILE // FRAME, (t + 1) * Q_TILE // FRAME)
        tops = jnp.zeros((Q_TILE, 128), jnp.float32)
        totals = jnp.zeros((Q_TILE, 128), jnp.float32)
        for h in range(HEADS):
            cols = slice(h * HEAD_DIM, (h + 1) * HEAD_DIM)
            k_head = jnp.concatenate([ref[slot, 0, :, cols] for ref, slot in blocks], axis=0)
            v_head = jnp.concatenate([ref[slot, 1, :, cols] for ref, slot in blocks], axis=0)
            k_wide = jnp.concatenate([k_head, bias_ref[...]], axis=1)
            v_wide = jnp.concatenate([v_head, ones], axis=1)
            q_head = q_ref[frames_at, :, cols].reshape(Q_TILE, HEAD_DIM)
            q_wide = jnp.concatenate([q_head, hot_ref[at, :]], axis=1)
            scores = lax.dot_general(
                q_wide, k_wide, (((1,), (1,)), ((), ())), preferred_element_type=jnp.float32
            )
            top = jnp.broadcast_to(jnp.max(scores, axis=1, keepdims=True), (Q_TILE, 128))
            if has_state:
                before = max_in[h, at, :]
                top = jnp.maximum(top, before)
            else:
                top = jnp.maximum(top, FLOOR)
            weights = jnp.exp2((scores - jnp.tile(top, (1, keys_n // 128))) * EXP2_SCALE).astype(
                jnp.bfloat16
            )
            both = jnp.dot(weights, v_wide, preferred_element_type=jnp.float32)
            acc, total = both[:, :HEAD_DIM], both[:, HEAD_DIM:]
            if has_state:
                fade = jnp.exp2((before - top) * EXP2_SCALE)
                acc = acc + acc_in[at, cols] * fade
                total = total + sum_in[h, at, :] * fade
            if not last:
                outs[0][at, cols] = acc
                outs[1][h, at, :] = top
                outs[2][h, at, :] = total
            else:
                tops = jnp.where(lanes == h, top, tops)
                totals = jnp.where(lanes == h, total, totals)
                mean = (acc * (1.0 / jnp.maximum(total, 1e-30))).astype(jnp.bfloat16)
                outs[0][frames_at, :, cols] = mean.reshape(Q_TILE // FRAME, FRAME, HEAD_DIM)
        if last:
            packed, slot = jnp.zeros((Q_TILE, 128), jnp.float32), 0
            for value, count in ((tops, TOP_PARTS), (totals, TOTAL_PARTS)):
                for _ in range(count):
                    part = value.astype(jnp.bfloat16).astype(jnp.float32)
                    value = value - part
                    packed = packed + (pltpu.roll(part, slot * 8, 1) if slot else part)
                    slot += 1
            outs[0][frames_at, :, WIDE:] = packed.astype(jnp.bfloat16).reshape(
                Q_TILE // FRAME, FRAME, STATS
            )


def attend_call(place, counts, q_all, kv, offsets, state, last):
    rows = COLUMNS * FRAME
    keys_n = sum(1 if kind == "half" else 2 for kind, _, _ in offsets) * FRAME
    if last:
        out_shape = jax.ShapeDtypeStruct((COLUMNS, FRAME, WIDE + STATS), jnp.bfloat16)
        out_specs = pl.BlockSpec(memory_space=pltpu.VMEM)
    else:
        out_shape = [
            jax.ShapeDtypeStruct((rows, WIDE), jnp.float32),
            jax.ShapeDtypeStruct((HEADS, rows, 128), jnp.float32),
            jax.ShapeDtypeStruct((HEADS, rows, 128), jnp.float32),
        ]
        out_specs = [pl.BlockSpec(memory_space=pltpu.VMEM)] * 3
    vmem = pl.BlockSpec(memory_space=pltpu.VMEM)
    smem = pl.BlockSpec(memory_space=pltpu.SMEM)
    flops = 2 * 2 * rows * keys_n * WIDE
    return pl.pallas_call(
        functools.partial(attend, offsets, state is not None, last),
        out_shape=out_shape,
        in_specs=[smem, smem] + [vmem] * (1 + len(kv) + (3 if state is not None else 0)),
        out_specs=out_specs,
        scratch_shapes=[
            pltpu.VMEM((keys_n, 128), jnp.bfloat16),
            pltpu.VMEM((rows, 128), jnp.bfloat16),
        ],
        compiler_params=pltpu.CompilerParams(vmem_limit_bytes=24 * 2**20),
        cost_estimate=pl.CostEstimate(
            flops=flops, bytes_accessed=4 * 2**20, transcendentals=rows * keys_n * HEADS
        ),
        name="attend_last" if last else "attend_first",
    )(place, counts, q_all, *kv, *(state if state is not None else ()))


def project(tp_count, place_ref, counts_ref, parts_ref, wo_ref, send_ref, keep_ref, att_ref):
    plane, column, core, tp = place_ref[0], place_ref[1], place_ref[2], place_ref[3]
    frame = (plane * COLUMNS + column) * 2 + core
    rows = lax.broadcasted_iota(jnp.int32, (FRAME, 1), 0)
    live = rows < counts_ref[frame]

    def part(stats, i):
        return pltpu.roll(stats, 128 - 8 * i, 1) if i else stats

    tops, totals = [], []
    for j in range(COLUMNS):
        stats = parts_ref[j, :, WIDE:].astype(jnp.float32)
        tops.append(sum(part(stats, i) for i in range(1, TOP_PARTS)) + stats)
        totals.append(sum(part(stats, TOP_PARTS + i) for i in range(TOTAL_PARTS)))
    top = functools.reduce(jnp.maximum, tops)
    shares = [n * jnp.exp2((m - top) * EXP2_SCALE) for m, n in zip(tops, totals)]
    total = functools.reduce(jnp.add, shares)
    shares = [jnp.where(live, share / total, 0.0) for share in shares]
    for h in range(HEADS):
        cols = slice(h * HEAD_DIM, (h + 1) * HEAD_DIM)
        out = functools.reduce(
            jnp.add,
            [
                parts_ref[j, :, cols].astype(jnp.float32) * shares[j][:, h : h + 1]
                for j in range(COLUMNS)
            ],
        )
        att_ref[:, cols] = out.astype(jnp.bfloat16)
    half = FRAME // tp_count
    mine = pl.ds(pl.multiple_of(tp * half, half), half)
    theirs = pl.ds(pl.multiple_of((1 - tp) * half, half), half)
    att = jnp.concatenate([att_ref[theirs, :], att_ref[mine, :]], axis=0)
    step = 512
    for n in range(0, wo_ref.shape[1], step):
        out = jnp.dot(att, wo_ref[:, n : n + step], preferred_element_type=jnp.float32)
        send_ref[:, n : n + step] = out[:half].astype(jnp.bfloat16)
        keep_ref[:, n : n + step] = out[half:]


def project_call(place, counts, parts, wo):
    vmem = pl.BlockSpec(memory_space=pltpu.VMEM)
    smem = pl.BlockSpec(memory_space=pltpu.SMEM)
    width = wo.shape[1]
    return pl.pallas_call(
        functools.partial(project, 2),
        out_shape=[
            jax.ShapeDtypeStruct((FRAME // 2, width), jnp.bfloat16),
            jax.ShapeDtypeStruct((FRAME // 2, width), jnp.float32),
        ],
        in_specs=[smem, smem, vmem, vmem],
        out_specs=[vmem, vmem],
        scratch_shapes=[pltpu.VMEM((FRAME, WIDE), jnp.bfloat16)],
        compiler_params=pltpu.CompilerParams(vmem_limit_bytes=24 * 2**20),
        name="project",
    )(place, counts, parts, wo)


SWAP = [(0, 1), (1, 0)]


def split_ring(distance):
    return [
        (z * 2 + c, (z + (distance if c == 0 else -distance)) % PLANES * 2 + c)
        for z in range(PLANES)
        for c in range(2)
    ]


def on_device(queries, keys, values, wo, frame_tokens):
    place = jnp.stack(
        [
            lax.axis_index("z"),
            lax.axis_index("xh") * 4 + lax.axis_index("y"),
            lax.axis_index("core"),
            lax.axis_index("tp"),
        ]
    ).astype(jnp.int32)
    own = jnp.stack([keys, values])
    own2 = jnp.stack([own, lax.ppermute(own, "core", SWAP)])
    zc = ("z", "core")
    near = lax.ppermute(own2, zc, split_ring(1))
    second = lax.ppermute(own2, zc, split_ring(2))
    q_all = lax.all_to_all(
        jnp.broadcast_to(queries[None], (COLUMNS, FRAME, WIDE)), ("xh", "y"), 0, 0, tiled=True
    )
    second, q_all = lax.optimization_barrier((second, q_all))
    third = lax.ppermute(second, zc, split_ring(1))
    fourth = lax.ppermute(second[:1], zc, split_ring(2))
    near_o = lax.ppermute(near, "core", SWAP)
    second_o = lax.ppermute(second, "core", SWAP)
    third_o = lax.ppermute(third, "core", SWAP)
    fourth_o = lax.ppermute(fourth, "core", SWAP)
    first = [own2, near, near_o, second, second_o]
    first_off = [
        ("both", 0, False),
        ("both", 1, False),
        ("both", 1, True),
        ("both", 2, False),
        ("both", 2, True),
    ]
    rest = [third, third_o, fourth, fourth_o]
    rest_off = [("both", 3, False), ("both", 3, True), ("half", 4, False), ("half", 4, True)]
    state = attend_call(place, frame_tokens, q_all, first, first_off, None, False)
    partial = attend_call(place, frame_tokens, q_all, rest, rest_off, state, True)
    parts = lax.all_to_all(partial, ("xh", "y"), 0, 0, tiled=True)
    send, keep = project_call(place, frame_tokens, parts, wo)
    got = lax.ppermute(send, "tp", SWAP)
    return (keep + got.astype(jnp.float32)).astype(jnp.bfloat16)


def solution(mesh):
    fine = Mesh(mesh.devices.reshape(PLANES, 2, 4, 2, 2), CTX + ("tp",))
    in_specs = (P(CTX, "tp"), P(CTX, "tp"), P(CTX, "tp"), P("tp", None), P())
    out_specs = P(CTX + ("tp",), None)
    return jax.shard_map(
        on_device, mesh=fine, in_specs=in_specs, out_specs=out_specs, check_vma=False
    )
```

```python
import functools
import math

import jax
import jax.numpy as jnp
from jax import lax
from jax.experimental import pallas as pl
from jax.experimental.pallas import tpu as pltpu
from jax.sharding import Mesh, PartitionSpec as P

HEAD_DIM = 128
FRAME = 64
PLANES = 8
COLUMNS = 8
HEADS = 6
WIDE = HEADS * HEAD_DIM
STATS = 128
TOP_PARTS, TOTAL_PARTS = 3, 2
Q_TILE = 256
CTX = ("z", "xh", "y", "core")
MASKED = -(2.0**24)
FLOOR = -(2.0**22)
EXP2_SCALE = math.log2(math.e) / math.sqrt(HEAD_DIM)


def fill_bias(bias_ref, frames, counts_ref, my_plane, my_core):
    rows = lax.broadcasted_iota(jnp.int32, (FRAME, 128), 0)
    lanes = lax.broadcasted_iota(jnp.int32, (FRAME, 128), 1)
    query_frames = (my_plane * COLUMNS + lanes) * 2 + my_core
    for i, frame in enumerate(frames):
        allowed = (rows < counts_ref[frame]) & (frame <= query_frames)
        bias_ref[i * FRAME : (i + 1) * FRAME, :] = jnp.where(allowed, 0.0, MASKED).astype(
            jnp.bfloat16
        )


def block_frame(place, offset, other):
    plane, column, core = place
    block_plane = lax.rem(plane + offset + PLANES, PLANES)
    return (block_plane * COLUMNS + column) * 2 + (1 - core if other else core)


def attend(offsets, has_state, last, *refs):
    place_ref, counts_ref, q_ref, *refs = refs
    kv_refs, refs = refs[: len(offsets)], refs[len(offsets) :]
    if has_state:
        acc_in, max_in, sum_in, *refs = refs
    outs, (bias_ref, hot_ref) = refs[:-2], refs[-2:]
    place = plane, column, core = place_ref[0], place_ref[1], place_ref[2]
    sign = 2 * core - 1
    blocks, frames = [], []
    for ref, (kind, distance, other_sender) in zip(kv_refs, offsets):
        direction = -sign if other_sender else sign
        for slot in range(2):
            if kind == "half":
                break
            blocks.append((ref, slot))
            frames.append(block_frame(place, direction * distance, (slot == 1) != other_sender))
        if kind == "half":
            blocks.append((ref, 0))
            frames.append(block_frame(place, distance, other_sender))
    fill_bias(bias_ref, frames, counts_ref, plane, core)
    rows = lax.broadcasted_iota(jnp.int32, (FRAME, 128), 1)
    for j in range(COLUMNS):
        hot_ref[j * FRAME : (j + 1) * FRAME, :] = jnp.where(rows == j, 1.0, 0.0).astype(jnp.bfloat16)
    keys_n = len(blocks) * FRAME
    ones = jnp.ones((keys_n, 128), jnp.bfloat16)
    lanes = lax.broadcasted_iota(jnp.int32, (Q_TILE, 128), 1)
    for t in range(COLUMNS * FRAME // Q_TILE):
        at = slice(t * Q_TILE, (t + 1) * Q_TILE)
        frames_at = slice(t * Q_TILE // FRAME, (t + 1) * Q_TILE // FRAME)
        tops = jnp.zeros((Q_TILE, 128), jnp.float32)
        totals = jnp.zeros((Q_TILE, 128), jnp.float32)
        for h in range(HEADS):
            cols = slice(h * HEAD_DIM, (h + 1) * HEAD_DIM)
            k_head = jnp.concatenate([ref[slot, 0, :, cols] for ref, slot in blocks], axis=0)
            v_head = jnp.concatenate([ref[slot, 1, :, cols] for ref, slot in blocks], axis=0)
            k_wide = jnp.concatenate([k_head, bias_ref[...]], axis=1)
            v_wide = jnp.concatenate([v_head, ones], axis=1)
            q_head = q_ref[frames_at, :, cols].reshape(Q_TILE, HEAD_DIM)
            q_wide = jnp.concatenate([q_head, hot_ref[at, :]], axis=1)
            scores = lax.dot_general(
                q_wide, k_wide, (((1,), (1,)), ((), ())), preferred_element_type=jnp.float32
            )
            top = jnp.broadcast_to(jnp.max(scores, axis=1, keepdims=True), (Q_TILE, 128))
            if has_state:
                before = max_in[h, at, :]
                top = jnp.maximum(top, before)
            else:
                top = jnp.maximum(top, FLOOR)
            weights = jnp.exp2((scores - jnp.tile(top, (1, keys_n // 128))) * EXP2_SCALE).astype(
                jnp.bfloat16
            )
            both = jnp.dot(weights, v_wide, preferred_element_type=jnp.float32)
            acc, total = both[:, :HEAD_DIM], both[:, HEAD_DIM:]
            if has_state:
                fade = jnp.exp2((before - top) * EXP2_SCALE)
                acc = acc + acc_in[at, cols] * fade
                total = total + sum_in[h, at, :] * fade
            if not last:
                outs[0][at, cols] = acc
                outs[1][h, at, :] = top
                outs[2][h, at, :] = total
            else:
                tops = jnp.where(lanes == h, top, tops)
                totals = jnp.where(lanes == h, total, totals)
                mean = (acc * (1.0 / jnp.maximum(total, 1e-30))).astype(jnp.bfloat16)
                outs[0][frames_at, :, cols] = mean.reshape(Q_TILE // FRAME, FRAME, HEAD_DIM)
        if last:
            packed, slot = jnp.zeros((Q_TILE, 128), jnp.float32), 0
            for value, count in ((tops, TOP_PARTS), (totals, TOTAL_PARTS)):
                for _ in range(count):
                    part = value.astype(jnp.bfloat16).astype(jnp.float32)
                    value = value - part
                    packed = packed + (pltpu.roll(part, slot * 8, 1) if slot else part)
                    slot += 1
            outs[0][frames_at, :, WIDE:] = packed.astype(jnp.bfloat16).reshape(
                Q_TILE // FRAME, FRAME, STATS
            )


def attend_call(place, counts, q_all, kv, offsets, state, last):
    rows = COLUMNS * FRAME
    keys_n = sum(1 if kind == "half" else 2 for kind, _, _ in offsets) * FRAME
    if last:
        out_shape = jax.ShapeDtypeStruct((COLUMNS, FRAME, WIDE + STATS), jnp.bfloat16)
        out_specs = pl.BlockSpec(memory_space=pltpu.VMEM)
    else:
        out_shape = [
            jax.ShapeDtypeStruct((rows, WIDE), jnp.float32),
            jax.ShapeDtypeStruct((HEADS, rows, 128), jnp.float32),
            jax.ShapeDtypeStruct((HEADS, rows, 128), jnp.float32),
        ]
        out_specs = [pl.BlockSpec(memory_space=pltpu.VMEM)] * 3
    vmem = pl.BlockSpec(memory_space=pltpu.VMEM)
    smem = pl.BlockSpec(memory_space=pltpu.SMEM)
    flops = 2 * 2 * rows * keys_n * WIDE
    return pl.pallas_call(
        functools.partial(attend, offsets, state is not None, last),
        out_shape=out_shape,
        in_specs=[smem, smem] + [vmem] * (1 + len(kv) + (3 if state is not None else 0)),
        out_specs=out_specs,
        scratch_shapes=[
            pltpu.VMEM((keys_n, 128), jnp.bfloat16),
            pltpu.VMEM((rows, 128), jnp.bfloat16),
        ],
        compiler_params=pltpu.CompilerParams(vmem_limit_bytes=24 * 2**20),
        cost_estimate=pl.CostEstimate(
            flops=flops, bytes_accessed=4 * 2**20, transcendentals=rows * keys_n * HEADS
        ),
        name="attend_last" if last else "attend_first",
    )(place, counts, q_all, *kv, *(state if state is not None else ()))


def project(tp_count, place_ref, counts_ref, parts_ref, wo_ref, send_ref, keep_ref, att_ref):
    plane, column, core, tp = place_ref[0], place_ref[1], place_ref[2], place_ref[3]
    frame = (plane * COLUMNS + column) * 2 + core
    rows = lax.broadcasted_iota(jnp.int32, (FRAME, 1), 0)
    live = rows < counts_ref[frame]

    def part(stats, i):
        return pltpu.roll(stats, 128 - 8 * i, 1) if i else stats

    tops, totals = [], []
    for j in range(COLUMNS):
        stats = parts_ref[j, :, WIDE:].astype(jnp.float32)
        tops.append(sum(part(stats, i) for i in range(1, TOP_PARTS)) + stats)
        totals.append(sum(part(stats, TOP_PARTS + i) for i in range(TOTAL_PARTS)))
    top = functools.reduce(jnp.maximum, tops)
    shares = [n * jnp.exp2((m - top) * EXP2_SCALE) for m, n in zip(tops, totals)]
    total = functools.reduce(jnp.add, shares)
    shares = [jnp.where(live, share / total, 0.0) for share in shares]
    for h in range(HEADS):
        cols = slice(h * HEAD_DIM, (h + 1) * HEAD_DIM)
        out = functools.reduce(
            jnp.add,
            [
                parts_ref[j, :, cols].astype(jnp.float32) * shares[j][:, h : h + 1]
                for j in range(COLUMNS)
            ],
        )
        att_ref[:, cols] = out.astype(jnp.bfloat16)
    half = FRAME // tp_count
    mine = pl.ds(pl.multiple_of(tp * half, half), half)
    theirs = pl.ds(pl.multiple_of((1 - tp) * half, half), half)
    att = jnp.concatenate([att_ref[theirs, :], att_ref[mine, :]], axis=0)
    step = 512
    for n in range(0, wo_ref.shape[1], step):
        out = jnp.dot(att, wo_ref[:, n : n + step], preferred_element_type=jnp.float32)
        send_ref[:, n : n + step] = out[:half].astype(jnp.bfloat16)
        keep_ref[:, n : n + step] = out[half:]


def project_call(place, counts, parts, wo):
    vmem = pl.BlockSpec(memory_space=pltpu.VMEM)
    smem = pl.BlockSpec(memory_space=pltpu.SMEM)
    width = wo.shape[1]
    return pl.pallas_call(
        functools.partial(project, 2),
        out_shape=[
            jax.ShapeDtypeStruct((FRAME // 2, width), jnp.bfloat16),
            jax.ShapeDtypeStruct((FRAME // 2, width), jnp.float32),
        ],
        in_specs=[smem, smem, vmem, vmem],
        out_specs=[vmem, vmem],
        scratch_shapes=[pltpu.VMEM((FRAME, WIDE), jnp.bfloat16)],
        compiler_params=pltpu.CompilerParams(vmem_limit_bytes=24 * 2**20),
        name="project",
    )(place, counts, parts, wo)


SWAP = [(0, 1), (1, 0)]


def split_ring(distance):
    return [
        (z * 2 + c, (z + (distance if c == 0 else -distance)) % PLANES * 2 + c)
        for z in range(PLANES)
        for c in range(2)
    ]


def on_device(queries, keys, values, wo, frame_tokens):
    place = jnp.stack(
        [
            lax.axis_index("z"),
            lax.axis_index("xh") * 4 + lax.axis_index("y"),
            lax.axis_index("core"),
            lax.axis_index("tp"),
        ]
    ).astype(jnp.int32)
    own = jnp.stack([keys, values])
    own2 = jnp.stack([own, lax.ppermute(own, "core", SWAP)])
    zc = ("z", "core")
    queries, own2 = lax.optimization_barrier((queries, own2))
    second = lax.ppermute(own2, zc, split_ring(2))
    near = lax.ppermute(own2, zc, split_ring(1))
    q_all = lax.all_to_all(
        jnp.broadcast_to(queries[None], (COLUMNS, FRAME, WIDE)), ("xh", "y"), 0, 0, tiled=True
    )
    fourth = lax.ppermute(second[:1], zc, split_ring(2))
    third = lax.ppermute(second, zc, split_ring(1))
    near, second = lax.optimization_barrier((near, second))
    near_o = lax.ppermute(near, "core", SWAP)
    second_o = lax.ppermute(second, "core", SWAP)
    first = [own2, near, near_o, second, second_o]
    first_off = [
        ("both", 0, False),
        ("both", 1, False),
        ("both", 1, True),
        ("both", 2, False),
        ("both", 2, True),
    ]
    state = attend_call(place, frame_tokens, q_all, first, first_off, None, False)
    third, fourth, state = lax.optimization_barrier((third, fourth, state))
    third_o = lax.ppermute(third, "core", SWAP)
    fourth_o = lax.ppermute(fourth, "core", SWAP)
    rest = [third, third_o, fourth, fourth_o]
    rest_off = [("both", 3, False), ("both", 3, True), ("half", 4, False), ("half", 4, True)]
    partial = attend_call(place, frame_tokens, q_all, rest, rest_off, state, True)
    parts = lax.all_to_all(partial, ("xh", "y"), 0, 0, tiled=True)
    send, keep = project_call(place, frame_tokens, parts, wo)
    got = lax.ppermute(send, "tp", SWAP)
    return (keep + got.astype(jnp.float32)).astype(jnp.bfloat16)


def solution(mesh):
    fine = Mesh(mesh.devices.reshape(PLANES, 2, 4, 2, 2), CTX + ("tp",))
    in_specs = (P(CTX, "tp"), P(CTX, "tp"), P(CTX, "tp"), P("tp", None), P())
    out_specs = P(CTX + ("tp",), None)
    return jax.shard_map(
        on_device, mesh=fine, in_specs=in_specs, out_specs=out_specs, check_vma=False
    )
```

```python
import functools
import math

import jax
import jax.numpy as jnp
from jax import lax
from jax.experimental import pallas as pl
from jax.experimental.pallas import tpu as pltpu
from jax.sharding import Mesh, PartitionSpec as P

HEAD_DIM = 128
FRAME = 64
PLANES = 8
COLUMNS = 8
HEADS = 6
WIDE = HEADS * HEAD_DIM
STATS = 16
SENT_ROWS = HEADS * FRAME + STATS
TOP_PARTS, TOTAL_PARTS = 3, 2
Q_TILE = 256
CTX = ("z", "xh", "y", "core")
MASKED = -(2.0**24)
FLOOR = -(2.0**22)
EXP2_SCALE = math.log2(math.e) / math.sqrt(HEAD_DIM)


def fill_bias(bias_ref, frames, counts_ref, my_plane, my_core):
    rows = lax.broadcasted_iota(jnp.int32, (FRAME, 128), 0)
    lanes = lax.broadcasted_iota(jnp.int32, (FRAME, 128), 1)
    query_frames = (my_plane * COLUMNS + lanes) * 2 + my_core
    for i, frame in enumerate(frames):
        allowed = (rows < counts_ref[frame]) & (frame <= query_frames)
        bias_ref[i * FRAME : (i + 1) * FRAME, :] = jnp.where(allowed, 0.0, MASKED).astype(
            jnp.bfloat16
        )


def block_frame(place, offset, other):
    plane, column, core = place
    block_plane = lax.rem(plane + offset + PLANES, PLANES)
    return (block_plane * COLUMNS + column) * 2 + (1 - core if other else core)


def attend(offsets, has_state, last, *refs):
    place_ref, counts_ref, q_ref, *refs = refs
    kv_refs, refs = refs[: len(offsets)], refs[len(offsets) :]
    if has_state:
        acc_in, max_in, sum_in, *refs = refs
    outs, (bias_ref, hot_ref) = refs[:-2], refs[-2:]
    place = plane, column, core = place_ref[0], place_ref[1], place_ref[2]
    sign = 2 * core - 1
    blocks, frames = [], []
    for ref, (kind, distance, other_sender) in zip(kv_refs, offsets):
        direction = -sign if other_sender else sign
        for slot in range(2):
            if kind == "half":
                break
            blocks.append((ref, slot))
            frames.append(block_frame(place, direction * distance, (slot == 1) != other_sender))
        if kind == "half":
            blocks.append((ref, 0))
            frames.append(block_frame(place, distance, other_sender))
    fill_bias(bias_ref, frames, counts_ref, plane, core)
    rows = lax.broadcasted_iota(jnp.int32, (FRAME, 128), 1)
    for j in range(COLUMNS):
        hot_ref[j * FRAME : (j + 1) * FRAME, :] = jnp.where(rows == j, 1.0, 0.0).astype(jnp.bfloat16)
    keys_n = len(blocks) * FRAME
    ones = jnp.ones((keys_n, 128), jnp.bfloat16)
    lanes = lax.broadcasted_iota(jnp.int32, (Q_TILE, 128), 1)
    for t in range(COLUMNS * FRAME // Q_TILE):
        at = slice(t * Q_TILE, (t + 1) * Q_TILE)
        frames_at = slice(t * Q_TILE // FRAME, (t + 1) * Q_TILE // FRAME)
        tops = jnp.zeros((Q_TILE, 128), jnp.float32)
        totals = jnp.zeros((Q_TILE, 128), jnp.float32)
        for h in range(HEADS):
            cols = slice(h * HEAD_DIM, (h + 1) * HEAD_DIM)
            k_head = jnp.concatenate([ref[slot, 0, :, cols] for ref, slot in blocks], axis=0)
            v_head = jnp.concatenate([ref[slot, 1, :, cols] for ref, slot in blocks], axis=0)
            k_wide = jnp.concatenate([k_head, bias_ref[...]], axis=1)
            v_wide = jnp.concatenate([v_head, ones], axis=1)
            q_head = q_ref[frames_at, :, cols].reshape(Q_TILE, HEAD_DIM)
            q_wide = jnp.concatenate([q_head, hot_ref[at, :]], axis=1)
            scores = lax.dot_general(
                q_wide, k_wide, (((1,), (1,)), ((), ())), preferred_element_type=jnp.float32
            )
            top = jnp.broadcast_to(jnp.max(scores, axis=1, keepdims=True), (Q_TILE, 128))
            if has_state:
                before = max_in[h, at, :]
                top = jnp.maximum(top, before)
            else:
                top = jnp.maximum(top, FLOOR)
            weights = jnp.exp2((scores - jnp.tile(top, (1, keys_n // 128))) * EXP2_SCALE).astype(
                jnp.bfloat16
            )
            both = jnp.dot(weights, v_wide, preferred_element_type=jnp.float32)
            acc, total = both[:, :HEAD_DIM], both[:, HEAD_DIM:]
            if has_state:
                fade = jnp.exp2((before - top) * EXP2_SCALE)
                acc = acc + acc_in[at, cols] * fade
                total = total + sum_in[h, at, :] * fade
            if not last:
                outs[0][at, cols] = acc
                outs[1][h, at, :] = top
                outs[2][h, at, :] = total
            else:
                tops = jnp.where(lanes == h, top, tops)
                totals = jnp.where(lanes == h, total, totals)
                mean = (acc * (1.0 / jnp.maximum(total, 1e-30))).astype(jnp.bfloat16)
                head_rows = slice(h * FRAME, (h + 1) * FRAME)
                outs[0][frames_at, head_rows, :] = mean.reshape(Q_TILE // FRAME, FRAME, HEAD_DIM)
        if last:
            packed, slot = jnp.zeros((Q_TILE, 128), jnp.float32), 0
            for value, count in ((tops, TOP_PARTS), (totals, TOTAL_PARTS)):
                for _ in range(count):
                    part = value.astype(jnp.bfloat16).astype(jnp.float32)
                    value = value - part
                    packed = packed + (pltpu.roll(part, slot * HEADS, 1) if slot else part)
                    slot += 1
            packed = packed.reshape(Q_TILE // FRAME, FRAME, 128)
            for i in range(Q_TILE // FRAME):
                folded = packed[i, :STATS]
                for k in range(1, FRAME // STATS):
                    folded = folded + pltpu.roll(packed[i, k * STATS : (k + 1) * STATS], 32 * k, 1)
                outs[0][t * (Q_TILE // FRAME) + i, HEADS * FRAME :, :] = folded.astype(jnp.bfloat16)


def attend_call(place, counts, q_all, kv, offsets, state, last):
    rows = COLUMNS * FRAME
    keys_n = sum(1 if kind == "half" else 2 for kind, _, _ in offsets) * FRAME
    if last:
        out_shape = jax.ShapeDtypeStruct((COLUMNS, SENT_ROWS, HEAD_DIM), jnp.bfloat16)
        out_specs = pl.BlockSpec(memory_space=pltpu.VMEM)
    else:
        out_shape = [
            jax.ShapeDtypeStruct((rows, WIDE), jnp.float32),
            jax.ShapeDtypeStruct((HEADS, rows, 128), jnp.float32),
            jax.ShapeDtypeStruct((HEADS, rows, 128), jnp.float32),
        ]
        out_specs = [pl.BlockSpec(memory_space=pltpu.VMEM)] * 3
    vmem = pl.BlockSpec(memory_space=pltpu.VMEM)
    smem = pl.BlockSpec(memory_space=pltpu.SMEM)
    flops = 2 * 2 * rows * keys_n * WIDE
    return pl.pallas_call(
        functools.partial(attend, offsets, state is not None, last),
        out_shape=out_shape,
        in_specs=[smem, smem] + [vmem] * (1 + len(kv) + (3 if state is not None else 0)),
        out_specs=out_specs,
        scratch_shapes=[
            pltpu.VMEM((keys_n, 128), jnp.bfloat16),
            pltpu.VMEM((rows, 128), jnp.bfloat16),
        ],
        compiler_params=pltpu.CompilerParams(vmem_limit_bytes=24 * 2**20),
        cost_estimate=pl.CostEstimate(
            flops=flops, bytes_accessed=4 * 2**20, transcendentals=rows * keys_n * HEADS
        ),
        name="attend_last" if last else "attend_first",
    )(place, counts, q_all, *kv, *(state if state is not None else ()))


def project(own, place_ref, counts_ref, parts_ref, wo_ref, out_ref, share_ref):
    plane, column, core, tp = place_ref[0], place_ref[1], place_ref[2], place_ref[3]
    frame = (plane * COLUMNS + column) * 2 + core
    rows = lax.broadcasted_iota(jnp.int32, (FRAME, 1), 0)
    live = rows < counts_ref[frame]

    def part(stats, i):
        return pltpu.roll(stats, 128 - HEADS * i, 1) if i else stats

    tops, totals = [], []
    for j in range(COLUMNS):
        folded = parts_ref[j, HEADS * FRAME :, :].astype(jnp.float32)
        stats = jnp.concatenate(
            [folded] + [pltpu.roll(folded, 128 - 32 * k, 1) for k in range(1, FRAME // STATS)], axis=0
        )
        tops.append(sum(part(stats, i) for i in range(1, TOP_PARTS)) + stats)
        totals.append(sum(part(stats, TOP_PARTS + i) for i in range(TOTAL_PARTS)))
    top = functools.reduce(jnp.maximum, tops)
    shares = [n * jnp.exp2((m - top) * EXP2_SCALE) for m, n in zip(tops, totals)]
    total = functools.reduce(jnp.add, shares)
    for j, share in enumerate(shares):
        share_ref[j] = jnp.where(live, share / total, 0.0)
    half = FRAME // 2
    first = (tp if own else 1 - tp) * half
    heads = []
    for h in range(HEADS):
        at = pl.ds(pl.multiple_of(h * FRAME + first, half), half)
        share_at = pl.ds(pl.multiple_of(first, half), half)
        heads.append(
            functools.reduce(
                jnp.add,
                [
                    parts_ref[j, at, :].astype(jnp.float32) * share_ref[j, share_at, h : h + 1]
                    for j in range(COLUMNS)
                ],
            ).astype(jnp.bfloat16)
        )
    att = jnp.concatenate(heads, axis=1)
    step = 512
    for n in range(0, wo_ref.shape[1], step):
        out_ref[:, n : n + step] = jnp.dot(
            att, wo_ref[:, n : n + step], preferred_element_type=jnp.float32
        ).astype(out_ref.dtype)


def project_call(place, counts, parts, wo, own):
    vmem = pl.BlockSpec(memory_space=pltpu.VMEM)
    smem = pl.BlockSpec(memory_space=pltpu.SMEM)
    return pl.pallas_call(
        functools.partial(project, own),
        out_shape=jax.ShapeDtypeStruct(
            (FRAME // 2, wo.shape[1]), jnp.float32 if own else jnp.bfloat16
        ),
        in_specs=[smem, smem, vmem, vmem],
        out_specs=vmem,
        scratch_shapes=[pltpu.VMEM((COLUMNS, FRAME, 128), jnp.float32)],
        compiler_params=pltpu.CompilerParams(vmem_limit_bytes=24 * 2**20),
        name="project_own" if own else "project_partner",
    )(place, counts, parts, wo)


SWAP = [(0, 1), (1, 0)]


def split_ring(distance):
    return [
        (z * 2 + c, (z + (distance if c == 0 else -distance)) % PLANES * 2 + c)
        for z in range(PLANES)
        for c in range(2)
    ]


def on_device(queries, keys, values, wo, frame_tokens):
    place = jnp.stack(
        [
            lax.axis_index("z"),
            lax.axis_index("xh") * 4 + lax.axis_index("y"),
            lax.axis_index("core"),
            lax.axis_index("tp"),
        ]
    ).astype(jnp.int32)
    own = jnp.stack([keys, values])
    own2 = jnp.stack([own, lax.ppermute(own, "core", SWAP)])
    zc = ("z", "core")
    queries, own2 = lax.optimization_barrier((queries, own2))
    second = lax.ppermute(own2, zc, split_ring(2))
    near = lax.ppermute(own2, zc, split_ring(1))
    q_all = lax.all_to_all(
        jnp.broadcast_to(queries[None], (COLUMNS, FRAME, WIDE)), ("xh", "y"), 0, 0, tiled=True
    )
    fourth = lax.ppermute(second[:1], zc, split_ring(2))
    third = lax.ppermute(second, zc, split_ring(1))
    near, second = lax.optimization_barrier((near, second))
    near_o = lax.ppermute(near, "core", SWAP)
    second_o = lax.ppermute(second, "core", SWAP)
    first = [own2, near, near_o, second, second_o]
    first_off = [
        ("both", 0, False),
        ("both", 1, False),
        ("both", 1, True),
        ("both", 2, False),
        ("both", 2, True),
    ]
    state = attend_call(place, frame_tokens, q_all, first, first_off, None, False)
    third, fourth, state = lax.optimization_barrier((third, fourth, state))
    third_o = lax.ppermute(third, "core", SWAP)
    fourth_o = lax.ppermute(fourth, "core", SWAP)
    rest = [third, third_o, fourth, fourth_o]
    rest_off = [("both", 3, False), ("both", 3, True), ("half", 4, False), ("half", 4, True)]
    partial = attend_call(place, frame_tokens, q_all, rest, rest_off, state, True)
    parts = lax.all_to_all(partial, ("xh", "y"), 0, 0, tiled=True)
    got = lax.ppermute(project_call(place, frame_tokens, parts, wo, False), "tp", SWAP)
    keep = project_call(place, frame_tokens, parts, wo, True)
    return (keep + got.astype(jnp.float32)).astype(jnp.bfloat16)


def solution(mesh):
    fine = Mesh(mesh.devices.reshape(PLANES, 2, 4, 2, 2), CTX + ("tp",))
    in_specs = (P(CTX, "tp"), P(CTX, "tp"), P(CTX, "tp"), P("tp", None), P())
    out_specs = P(CTX + ("tp",), None)
    return jax.shard_map(
        on_device, mesh=fine, in_specs=in_specs, out_specs=out_specs, check_vma=False
    )
```

```python
import functools
import math

import jax
import jax.numpy as jnp
from jax import lax
from jax.experimental import pallas as pl
from jax.experimental.pallas import tpu as pltpu
from jax.sharding import Mesh, PartitionSpec as P

HEAD_DIM = 128
FRAME = 64
PLANES = 8
COLUMNS = 8
HEADS = 6
WIDE = HEADS * HEAD_DIM
STATS = 16
SENT_ROWS = HEADS * FRAME + STATS
TOP_PARTS, TOTAL_PARTS = 3, 2
Q_TILE = 256
CTX = ("z", "xh", "y", "core")
MASKED = -(2.0**24)
FLOOR = -(2.0**22)
EXP2_SCALE = math.log2(math.e) / math.sqrt(HEAD_DIM)


def fill_bias(bias_ref, frames, counts_ref, my_plane, my_core):
    rows = lax.broadcasted_iota(jnp.int32, (FRAME, 128), 0)
    lanes = lax.broadcasted_iota(jnp.int32, (FRAME, 128), 1)
    query_frames = (my_plane * COLUMNS + lanes) * 2 + my_core
    for i, frame in enumerate(frames):
        allowed = (rows < counts_ref[frame]) & (frame <= query_frames)
        bias_ref[i * FRAME : (i + 1) * FRAME, :] = jnp.where(allowed, 0.0, MASKED).astype(
            jnp.bfloat16
        )


def block_frame(place, offset, other):
    plane, column, core = place
    block_plane = lax.rem(plane + offset + PLANES, PLANES)
    return (block_plane * COLUMNS + column) * 2 + (1 - core if other else core)


def attend(offsets, has_state, last, *refs):
    place_ref, counts_ref, q_ref, *refs = refs
    kv_refs, refs = refs[: len(offsets)], refs[len(offsets) :]
    if has_state:
        acc_in, max_in, sum_in, *refs = refs
    outs, (bias_ref, hot_ref) = refs[:-2], refs[-2:]
    place = plane, column, core = place_ref[0], place_ref[1], place_ref[2]
    sign = 2 * core - 1
    blocks, frames = [], []
    for ref, (kind, distance, other_sender) in zip(kv_refs, offsets):
        direction = -sign if other_sender else sign
        for slot in range(2):
            if kind == "half":
                break
            blocks.append((ref, slot))
            frames.append(block_frame(place, direction * distance, (slot == 1) != other_sender))
        if kind == "half":
            blocks.append((ref, 0))
            frames.append(block_frame(place, distance, other_sender))
    fill_bias(bias_ref, frames, counts_ref, plane, core)
    rows = lax.broadcasted_iota(jnp.int32, (FRAME, 128), 1)
    for j in range(COLUMNS):
        hot_ref[j * FRAME : (j + 1) * FRAME, :] = jnp.where(rows == j, 1.0, 0.0).astype(jnp.bfloat16)
    keys_n = len(blocks) * FRAME
    ones = jnp.ones((keys_n, 128), jnp.bfloat16)
    lanes = lax.broadcasted_iota(jnp.int32, (Q_TILE, 128), 1)
    for t in range(COLUMNS * FRAME // Q_TILE):
        at = slice(t * Q_TILE, (t + 1) * Q_TILE)
        frames_at = slice(t * Q_TILE // FRAME, (t + 1) * Q_TILE // FRAME)
        tops = jnp.zeros((Q_TILE, 128), jnp.float32)
        totals = jnp.zeros((Q_TILE, 128), jnp.float32)
        for h in range(HEADS):
            cols = slice(h * HEAD_DIM, (h + 1) * HEAD_DIM)
            k_head = jnp.concatenate([ref[slot, 0, :, cols] for ref, slot in blocks], axis=0)
            v_head = jnp.concatenate([ref[slot, 1, :, cols] for ref, slot in blocks], axis=0)
            k_wide = jnp.concatenate([k_head, bias_ref[...]], axis=1)
            v_wide = jnp.concatenate([v_head, ones], axis=1)
            q_head = q_ref[frames_at, :, cols].reshape(Q_TILE, HEAD_DIM)
            q_wide = jnp.concatenate([q_head, hot_ref[at, :]], axis=1)
            scores = lax.dot_general(
                q_wide, k_wide, (((1,), (1,)), ((), ())), preferred_element_type=jnp.float32
            )
            top = jnp.broadcast_to(jnp.max(scores, axis=1, keepdims=True), (Q_TILE, 128))
            if has_state:
                before = max_in[h, at, :]
                top = jnp.maximum(top, before)
            else:
                top = jnp.maximum(top, FLOOR)
            weights = jnp.exp2((scores - jnp.tile(top, (1, keys_n // 128))) * EXP2_SCALE).astype(
                jnp.bfloat16
            )
            both = jnp.dot(weights, v_wide, preferred_element_type=jnp.float32)
            acc, total = both[:, :HEAD_DIM], both[:, HEAD_DIM:]
            if has_state:
                fade = jnp.exp2((before - top) * EXP2_SCALE)
                acc = acc + acc_in[at, cols] * fade
                total = total + sum_in[h, at, :] * fade
            if not last:
                outs[0][at, cols] = acc
                outs[1][h, at, :] = top
                outs[2][h, at, :] = total
            else:
                tops = jnp.where(lanes == h, top, tops)
                totals = jnp.where(lanes == h, total, totals)
                mean = (acc * (1.0 / jnp.maximum(total, 1e-30))).astype(jnp.bfloat16)
                head_rows = slice(h * FRAME, (h + 1) * FRAME)
                outs[0][frames_at, head_rows, :] = mean.reshape(Q_TILE // FRAME, FRAME, HEAD_DIM)
        if last:
            packed, slot = jnp.zeros((Q_TILE, 128), jnp.float32), 0
            for value, count in ((tops, TOP_PARTS), (totals, TOTAL_PARTS)):
                for _ in range(count):
                    part = value.astype(jnp.bfloat16).astype(jnp.float32)
                    value = value - part
                    packed = packed + (pltpu.roll(part, slot * HEADS, 1) if slot else part)
                    slot += 1
            packed = packed.reshape(Q_TILE // FRAME, FRAME, 128)
            for i in range(Q_TILE // FRAME):
                folded = packed[i, :STATS]
                for k in range(1, FRAME // STATS):
                    folded = folded + pltpu.roll(packed[i, k * STATS : (k + 1) * STATS], 32 * k, 1)
                outs[0][t * (Q_TILE // FRAME) + i, HEADS * FRAME :, :] = folded.astype(jnp.bfloat16)


def attend_call(place, counts, q_all, kv, offsets, state, last):
    rows = COLUMNS * FRAME
    keys_n = sum(1 if kind == "half" else 2 for kind, _, _ in offsets) * FRAME
    if last:
        out_shape = jax.ShapeDtypeStruct((COLUMNS, SENT_ROWS, HEAD_DIM), jnp.bfloat16)
        out_specs = pl.BlockSpec(memory_space=pltpu.VMEM)
    else:
        out_shape = [
            jax.ShapeDtypeStruct((rows, WIDE), jnp.float32),
            jax.ShapeDtypeStruct((HEADS, rows, 128), jnp.float32),
            jax.ShapeDtypeStruct((HEADS, rows, 128), jnp.float32),
        ]
        out_specs = [pl.BlockSpec(memory_space=pltpu.VMEM)] * 3
    vmem = pl.BlockSpec(memory_space=pltpu.VMEM)
    smem = pl.BlockSpec(memory_space=pltpu.SMEM)
    flops = 2 * 2 * rows * keys_n * WIDE
    return pl.pallas_call(
        functools.partial(attend, offsets, state is not None, last),
        out_shape=out_shape,
        in_specs=[smem, smem] + [vmem] * (1 + len(kv) + (3 if state is not None else 0)),
        out_specs=out_specs,
        scratch_shapes=[
            pltpu.VMEM((keys_n, 128), jnp.bfloat16),
            pltpu.VMEM((rows, 128), jnp.bfloat16),
        ],
        compiler_params=pltpu.CompilerParams(vmem_limit_bytes=24 * 2**20),
        cost_estimate=pl.CostEstimate(
            flops=flops, bytes_accessed=4 * 2**20, transcendentals=rows * keys_n * HEADS
        ),
        name="attend_last" if last else "attend_first",
    )(place, counts, q_all, *kv, *(state if state is not None else ()))


def project(own, place_ref, counts_ref, parts_ref, wo_ref, out_ref, share_ref):
    plane, column, core, tp = place_ref[0], place_ref[1], place_ref[2], place_ref[3]
    frame = (plane * COLUMNS + column) * 2 + core
    rows = lax.broadcasted_iota(jnp.int32, (FRAME, 1), 0)
    live = rows < counts_ref[frame]

    def part(stats, i):
        return pltpu.roll(stats, 128 - HEADS * i, 1) if i else stats

    tops, totals = [], []
    for j in range(COLUMNS):
        folded = parts_ref[j, HEADS * FRAME :, :].astype(jnp.float32)
        stats = jnp.concatenate(
            [folded] + [pltpu.roll(folded, 128 - 32 * k, 1) for k in range(1, FRAME // STATS)], axis=0
        )
        tops.append(sum(part(stats, i) for i in range(1, TOP_PARTS)) + stats)
        totals.append(sum(part(stats, TOP_PARTS + i) for i in range(TOTAL_PARTS)))
    top = functools.reduce(jnp.maximum, tops)
    shares = [n * jnp.exp2((m - top) * EXP2_SCALE) for m, n in zip(tops, totals)]
    total = functools.reduce(jnp.add, shares)
    for j, share in enumerate(shares):
        share_ref[j] = jnp.where(live, share / total, 0.0)
    half = FRAME // 2
    first = (tp if own else 1 - tp) * half
    heads = []
    for h in range(HEADS):
        at = pl.ds(pl.multiple_of(h * FRAME + first, half), half)
        share_at = pl.ds(pl.multiple_of(first, half), half)
        heads.append(
            functools.reduce(
                jnp.add,
                [
                    parts_ref[j, at, :].astype(jnp.float32) * share_ref[j, share_at, h : h + 1]
                    for j in range(COLUMNS)
                ],
            ).astype(jnp.bfloat16)
        )
    att = jnp.concatenate(heads, axis=1)
    step = 512
    for n in range(0, wo_ref.shape[1], step):
        out_ref[:, n : n + step] = jnp.dot(
            att, wo_ref[:, n : n + step], preferred_element_type=jnp.float32
        ).astype(out_ref.dtype)


def project_call(place, counts, parts, wo, own):
    vmem = pl.BlockSpec(memory_space=pltpu.VMEM)
    smem = pl.BlockSpec(memory_space=pltpu.SMEM)
    return pl.pallas_call(
        functools.partial(project, own),
        out_shape=jax.ShapeDtypeStruct(
            (FRAME // 2, wo.shape[1]), jnp.float32 if own else jnp.bfloat16
        ),
        in_specs=[smem, smem, vmem, vmem],
        out_specs=vmem,
        scratch_shapes=[pltpu.VMEM((COLUMNS, FRAME, 128), jnp.float32)],
        compiler_params=pltpu.CompilerParams(vmem_limit_bytes=24 * 2**20),
        name="project_own" if own else "project_partner",
    )(place, counts, parts, wo)


SWAP = [(0, 1), (1, 0)]


def split_ring(distance):
    return [
        (z * 2 + c, (z + (distance if c == 0 else -distance)) % PLANES * 2 + c)
        for z in range(PLANES)
        for c in range(2)
    ]


def on_device(queries, keys, values, wo, frame_tokens):
    place = jnp.stack(
        [
            lax.axis_index("z"),
            lax.axis_index("xh") * 4 + lax.axis_index("y"),
            lax.axis_index("core"),
            lax.axis_index("tp"),
        ]
    ).astype(jnp.int32)
    own = jnp.stack([keys, values])
    own2 = jnp.stack([own, lax.ppermute(own, "core", SWAP)])
    zc = ("z", "core")
    queries, own2 = lax.optimization_barrier((queries, own2))
    second = lax.ppermute(own2, zc, split_ring(2))
    near = lax.ppermute(own2, zc, split_ring(1))
    q_all = lax.all_to_all(
        jnp.broadcast_to(queries[None], (COLUMNS, FRAME, WIDE)), ("xh", "y"), 0, 0, tiled=True
    )
    fourth = lax.ppermute(second[:1], zc, split_ring(2))
    third = lax.ppermute(second, zc, split_ring(1))
    near, q_all = lax.optimization_barrier((near, q_all))
    second_o = lax.ppermute(second, "core", SWAP)
    state = attend_call(
        place,
        frame_tokens,
        q_all,
        [own2, second, second_o],
        [("both", 0, False), ("both", 2, False), ("both", 2, True)],
        None,
        False,
    )
    near, third, fourth, state = lax.optimization_barrier((near, third, fourth, state))
    near_o = lax.ppermute(near, "core", SWAP)
    third_o = lax.ppermute(third, "core", SWAP)
    fourth_o = lax.ppermute(fourth, "core", SWAP)
    rest = [near, near_o, third, third_o, fourth, fourth_o]
    rest_off = [
        ("both", 1, False),
        ("both", 1, True),
        ("both", 3, False),
        ("both", 3, True),
        ("half", 4, False),
        ("half", 4, True),
    ]
    partial = attend_call(place, frame_tokens, q_all, rest, rest_off, state, True)
    parts = lax.all_to_all(partial, ("xh", "y"), 0, 0, tiled=True)
    got = lax.ppermute(project_call(place, frame_tokens, parts, wo, False), "tp", SWAP)
    keep = project_call(place, frame_tokens, parts, wo, True)
    return (keep + got.astype(jnp.float32)).astype(jnp.bfloat16)


def solution(mesh):
    fine = Mesh(mesh.devices.reshape(PLANES, 2, 4, 2, 2), CTX + ("tp",))
    in_specs = (P(CTX, "tp"), P(CTX, "tp"), P(CTX, "tp"), P("tp", None), P())
    out_specs = P(CTX + ("tp",), None)
    return jax.shard_map(
        on_device, mesh=fine, in_specs=in_specs, out_specs=out_specs, check_vma=False
    )
```

```python
import functools
import math

import jax
import jax.numpy as jnp
from jax import lax
from jax.experimental import pallas as pl
from jax.experimental.pallas import tpu as pltpu
from jax.sharding import Mesh, PartitionSpec as P

HEAD_DIM = 128
FRAME = 64
PLANES = 8
COLUMNS = 8
HEADS = 6
WIDE = HEADS * HEAD_DIM
STATS = 16
SENT_ROWS = HEADS * FRAME + STATS
TOP_PARTS, TOTAL_PARTS = 3, 2
Q_TILE = 256
CTX = ("z", "xh", "y", "core")
MASKED = -(2.0**24)
FLOOR = -(2.0**22)
EXP2_SCALE = math.log2(math.e) / math.sqrt(HEAD_DIM)


def fill_bias(bias_ref, frames, counts_ref, my_plane, my_core):
    rows = lax.broadcasted_iota(jnp.int32, (FRAME, 128), 0)
    lanes = lax.broadcasted_iota(jnp.int32, (FRAME, 128), 1)
    query_frames = (my_plane * COLUMNS + lanes) * 2 + my_core
    for i, frame in enumerate(frames):
        allowed = (rows < counts_ref[frame]) & (frame <= query_frames)
        bias_ref[i * FRAME : (i + 1) * FRAME, :] = jnp.where(allowed, 0.0, MASKED).astype(
            jnp.bfloat16
        )


def block_frame(place, offset, other):
    plane, column, core = place
    block_plane = lax.rem(plane + offset + PLANES, PLANES)
    return (block_plane * COLUMNS + column) * 2 + (1 - core if other else core)


def attend(offsets, has_state, last, *refs):
    place_ref, counts_ref, q_ref, *refs = refs
    kv_refs, refs = refs[: len(offsets)], refs[len(offsets) :]
    if has_state:
        acc_in, max_in, sum_in, *refs = refs
    outs, (bias_ref, hot_ref) = refs[:-2], refs[-2:]
    place = plane, column, core = place_ref[0], place_ref[1], place_ref[2]
    sign = 2 * core - 1
    blocks, frames = [], []
    for ref, (kind, distance, other_sender) in zip(kv_refs, offsets):
        direction = -sign if other_sender else sign
        for slot in range(2):
            if kind == "half":
                break
            blocks.append((ref, slot))
            frames.append(block_frame(place, direction * distance, (slot == 1) != other_sender))
        if kind == "half":
            blocks.append((ref, 0))
            frames.append(block_frame(place, distance, other_sender))
    fill_bias(bias_ref, frames, counts_ref, plane, core)
    rows = lax.broadcasted_iota(jnp.int32, (FRAME, 128), 1)
    for j in range(COLUMNS):
        hot_ref[j * FRAME : (j + 1) * FRAME, :] = jnp.where(rows == j, 1.0, 0.0).astype(jnp.bfloat16)
    keys_n = len(blocks) * FRAME
    ones = jnp.ones((keys_n, 128), jnp.bfloat16)
    lanes = lax.broadcasted_iota(jnp.int32, (Q_TILE, 128), 1)
    for t in range(COLUMNS * FRAME // Q_TILE):
        at = slice(t * Q_TILE, (t + 1) * Q_TILE)
        frames_at = slice(t * Q_TILE // FRAME, (t + 1) * Q_TILE // FRAME)
        tops = jnp.zeros((Q_TILE, 128), jnp.float32)
        totals = jnp.zeros((Q_TILE, 128), jnp.float32)
        for h in range(HEADS):
            cols = slice(h * HEAD_DIM, (h + 1) * HEAD_DIM)
            k_head = jnp.concatenate([ref[slot, 0, :, cols] for ref, slot in blocks], axis=0)
            v_head = jnp.concatenate([ref[slot, 1, :, cols] for ref, slot in blocks], axis=0)
            k_wide = jnp.concatenate([k_head, bias_ref[...]], axis=1)
            v_wide = jnp.concatenate([v_head, ones], axis=1)
            q_head = q_ref[frames_at, :, cols].reshape(Q_TILE, HEAD_DIM)
            q_wide = jnp.concatenate([q_head, hot_ref[at, :]], axis=1)
            scores = lax.dot_general(
                q_wide, k_wide, (((1,), (1,)), ((), ())), preferred_element_type=jnp.float32
            )
            top = jnp.broadcast_to(jnp.max(scores, axis=1, keepdims=True), (Q_TILE, 128))
            if has_state:
                before = max_in[h, at, :]
                top = jnp.maximum(top, before)
            else:
                top = jnp.maximum(top, FLOOR)
            weights = jnp.exp2((scores - jnp.tile(top, (1, keys_n // 128))) * EXP2_SCALE).astype(
                jnp.bfloat16
            )
            both = jnp.dot(weights, v_wide, preferred_element_type=jnp.float32)
            acc, total = both[:, :HEAD_DIM], both[:, HEAD_DIM:]
            if has_state:
                fade = jnp.exp2((before - top) * EXP2_SCALE)
                acc = acc + acc_in[at, cols] * fade
                total = total + sum_in[h, at, :] * fade
            if not last:
                outs[0][at, cols] = acc
                outs[1][h, at, :] = top
                outs[2][h, at, :] = total
            else:
                tops = jnp.where(lanes == h, top, tops)
                totals = jnp.where(lanes == h, total, totals)
                mean = (acc * (1.0 / jnp.maximum(total, 1e-30))).astype(jnp.bfloat16)
                head_rows = slice(h * FRAME, (h + 1) * FRAME)
                outs[0][frames_at, head_rows, :] = mean.reshape(Q_TILE // FRAME, FRAME, HEAD_DIM)
        if last:
            packed, slot = jnp.zeros((Q_TILE, 128), jnp.float32), 0
            for value, count in ((tops, TOP_PARTS), (totals, TOTAL_PARTS)):
                for _ in range(count):
                    part = value.astype(jnp.bfloat16).astype(jnp.float32)
                    value = value - part
                    packed = packed + (pltpu.roll(part, slot * HEADS, 1) if slot else part)
                    slot += 1
            packed = packed.reshape(Q_TILE // FRAME, FRAME, 128)
            for i in range(Q_TILE // FRAME):
                folded = packed[i, :STATS]
                for k in range(1, FRAME // STATS):
                    folded = folded + pltpu.roll(packed[i, k * STATS : (k + 1) * STATS], 32 * k, 1)
                outs[0][t * (Q_TILE // FRAME) + i, HEADS * FRAME :, :] = folded.astype(jnp.bfloat16)


def attend_call(place, counts, q_all, kv, offsets, state, last):
    rows = COLUMNS * FRAME
    keys_n = sum(1 if kind == "half" else 2 for kind, _, _ in offsets) * FRAME
    if last:
        out_shape = jax.ShapeDtypeStruct((COLUMNS, SENT_ROWS, HEAD_DIM), jnp.bfloat16)
        out_specs = pl.BlockSpec(memory_space=pltpu.VMEM)
    else:
        out_shape = [
            jax.ShapeDtypeStruct((rows, WIDE), jnp.float32),
            jax.ShapeDtypeStruct((HEADS, rows, 128), jnp.float32),
            jax.ShapeDtypeStruct((HEADS, rows, 128), jnp.float32),
        ]
        out_specs = [pl.BlockSpec(memory_space=pltpu.VMEM)] * 3
    vmem = pl.BlockSpec(memory_space=pltpu.VMEM)
    smem = pl.BlockSpec(memory_space=pltpu.SMEM)
    flops = 2 * 2 * rows * keys_n * WIDE
    return pl.pallas_call(
        functools.partial(attend, offsets, state is not None, last),
        out_shape=out_shape,
        in_specs=[smem, smem] + [vmem] * (1 + len(kv) + (3 if state is not None else 0)),
        out_specs=out_specs,
        scratch_shapes=[
            pltpu.VMEM((keys_n, 128), jnp.bfloat16),
            pltpu.VMEM((rows, 128), jnp.bfloat16),
        ],
        compiler_params=pltpu.CompilerParams(vmem_limit_bytes=24 * 2**20),
        cost_estimate=pl.CostEstimate(
            flops=flops, bytes_accessed=4 * 2**20, transcendentals=rows * keys_n * HEADS
        ),
        name="attend_last" if last else "attend_first",
    )(place, counts, q_all, *kv, *(state if state is not None else ()))


def project(own, place_ref, counts_ref, parts_ref, wo_ref, out_ref, share_ref):
    plane, column, core, tp = place_ref[0], place_ref[1], place_ref[2], place_ref[3]
    frame = (plane * COLUMNS + column) * 2 + core
    rows = lax.broadcasted_iota(jnp.int32, (FRAME, 1), 0)
    live = rows < counts_ref[frame]

    def part(stats, i):
        return pltpu.roll(stats, 128 - HEADS * i, 1) if i else stats

    tops, totals = [], []
    for j in range(COLUMNS):
        folded = parts_ref[j, HEADS * FRAME :, :].astype(jnp.float32)
        stats = jnp.concatenate(
            [folded] + [pltpu.roll(folded, 128 - 32 * k, 1) for k in range(1, FRAME // STATS)], axis=0
        )
        tops.append(sum(part(stats, i) for i in range(1, TOP_PARTS)) + stats)
        totals.append(sum(part(stats, TOP_PARTS + i) for i in range(TOTAL_PARTS)))
    top = functools.reduce(jnp.maximum, tops)
    shares = [n * jnp.exp2((m - top) * EXP2_SCALE) for m, n in zip(tops, totals)]
    total = functools.reduce(jnp.add, shares)
    for j, share in enumerate(shares):
        share_ref[j] = jnp.where(live, share / total, 0.0)
    half = FRAME // 2
    first = (tp if own else 1 - tp) * half
    heads = []
    for h in range(HEADS):
        at = pl.ds(pl.multiple_of(h * FRAME + first, half), half)
        share_at = pl.ds(pl.multiple_of(first, half), half)
        heads.append(
            functools.reduce(
                jnp.add,
                [
                    parts_ref[j, at, :].astype(jnp.float32) * share_ref[j, share_at, h : h + 1]
                    for j in range(COLUMNS)
                ],
            ).astype(jnp.bfloat16)
        )
    att = jnp.concatenate(heads, axis=1)
    step = 512
    for n in range(0, wo_ref.shape[1], step):
        out_ref[:, n : n + step] = jnp.dot(
            att, wo_ref[:, n : n + step], preferred_element_type=jnp.float32
        ).astype(out_ref.dtype)


def project_call(place, counts, parts, wo, own):
    vmem = pl.BlockSpec(memory_space=pltpu.VMEM)
    smem = pl.BlockSpec(memory_space=pltpu.SMEM)
    return pl.pallas_call(
        functools.partial(project, own),
        out_shape=jax.ShapeDtypeStruct(
            (FRAME // 2, wo.shape[1]), jnp.float32 if own else jnp.bfloat16
        ),
        in_specs=[smem, smem, vmem, vmem],
        out_specs=vmem,
        scratch_shapes=[pltpu.VMEM((COLUMNS, FRAME, 128), jnp.float32)],
        compiler_params=pltpu.CompilerParams(vmem_limit_bytes=24 * 2**20),
        name="project_own" if own else "project_partner",
    )(place, counts, parts, wo)


SWAP = [(0, 1), (1, 0)]


def split_ring(distance):
    return [
        (z * 2 + c, (z + (distance if c == 0 else -distance)) % PLANES * 2 + c)
        for z in range(PLANES)
        for c in range(2)
    ]


def on_device(queries, keys, values, wo, frame_tokens):
    place = jnp.stack(
        [
            lax.axis_index("z"),
            lax.axis_index("xh") * 4 + lax.axis_index("y"),
            lax.axis_index("core"),
            lax.axis_index("tp"),
        ]
    ).astype(jnp.int32)
    own = jnp.stack([keys, values])
    own2 = jnp.stack([own, lax.ppermute(own, "core", SWAP)])
    zc = ("z", "core")
    queries, own2 = lax.optimization_barrier((queries, own2))
    second = lax.ppermute(own2, zc, split_ring(2))
    near = lax.ppermute(own2, zc, split_ring(1))
    q_all = lax.all_to_all(
        jnp.broadcast_to(queries[None], (COLUMNS, FRAME, WIDE)), ("xh", "y"), 0, 0, tiled=True
    )
    fourth = lax.ppermute(second[:1], zc, split_ring(2))
    third = lax.ppermute(second, zc, split_ring(1))
    near, q_all = lax.optimization_barrier((near, q_all))
    second_o = lax.ppermute(second, "core", SWAP)
    state = attend_call(
        place,
        frame_tokens,
        q_all,
        [own2, near, second, second_o],
        [("both", 0, False), ("both", 1, False), ("both", 2, False), ("both", 2, True)],
        None,
        False,
    )
    near, third, fourth, state = lax.optimization_barrier((near, third, fourth, state))
    near_o = lax.ppermute(near, "core", SWAP)
    third_o = lax.ppermute(third, "core", SWAP)
    fourth_o = lax.ppermute(fourth, "core", SWAP)
    rest = [near_o, third, third_o, fourth, fourth_o]
    rest_off = [
        ("both", 1, True),
        ("both", 3, False),
        ("both", 3, True),
        ("half", 4, False),
        ("half", 4, True),
    ]
    partial = attend_call(place, frame_tokens, q_all, rest, rest_off, state, True)
    parts = lax.all_to_all(partial, ("xh", "y"), 0, 0, tiled=True)
    got = lax.ppermute(project_call(place, frame_tokens, parts, wo, False), "tp", SWAP)
    keep = project_call(place, frame_tokens, parts, wo, True)
    return (keep + got.astype(jnp.float32)).astype(jnp.bfloat16)


def solution(mesh):
    fine = Mesh(mesh.devices.reshape(PLANES, 2, 4, 2, 2), CTX + ("tp",))
    in_specs = (P(CTX, "tp"), P(CTX, "tp"), P(CTX, "tp"), P("tp", None), P())
    out_specs = P(CTX + ("tp",), None)
    return jax.shard_map(
        on_device, mesh=fine, in_specs=in_specs, out_specs=out_specs, check_vma=False
    )
```

```python
import functools
import math

import jax
import jax.numpy as jnp
from jax import lax
from jax.experimental import pallas as pl
from jax.experimental.pallas import tpu as pltpu
from jax.sharding import Mesh, PartitionSpec as P

HEAD_DIM = 128
FRAME = 64
PLANES = 8
COLUMNS = 8
HEADS = 6
WIDE = HEADS * HEAD_DIM
STATS = 16
SENT_ROWS = HEADS * FRAME + STATS
TOP_PARTS, TOTAL_PARTS = 3, 2
Q_TILE = 256
CTX = ("z", "xh", "y", "core")
MASKED = -(2.0**24)
FLOOR = -(2.0**22)
EXP2_SCALE = math.log2(math.e) / math.sqrt(HEAD_DIM)


def fill_bias(bias_ref, frames, counts_ref, my_plane, my_core):
    rows = lax.broadcasted_iota(jnp.int32, (FRAME, 128), 0)
    lanes = lax.broadcasted_iota(jnp.int32, (FRAME, 128), 1)
    query_frames = (my_plane * COLUMNS + lanes) * 2 + my_core
    for i, frame in enumerate(frames):
        allowed = (rows < counts_ref[frame]) & (frame <= query_frames)
        bias_ref[i * FRAME : (i + 1) * FRAME, :] = jnp.where(allowed, 0.0, MASKED).astype(
            jnp.bfloat16
        )


def block_frame(place, offset, other):
    plane, column, core = place
    block_plane = lax.rem(plane + offset + PLANES, PLANES)
    return (block_plane * COLUMNS + column) * 2 + (1 - core if other else core)


def attend(offsets, has_state, last, *refs):
    place_ref, counts_ref, q_ref, *refs = refs
    kv_refs, refs = refs[: len(offsets)], refs[len(offsets) :]
    if has_state:
        acc_in, max_in, sum_in, *refs = refs
    outs, (bias_ref, hot_ref) = refs[:-2], refs[-2:]
    place = plane, column, core = place_ref[0], place_ref[1], place_ref[2]
    sign = 2 * core - 1
    blocks, frames = [], []
    for ref, (kind, distance, other_sender) in zip(kv_refs, offsets):
        direction = -sign if other_sender else sign
        for slot in range(2):
            if kind == "half":
                break
            blocks.append((ref, slot))
            frames.append(block_frame(place, direction * distance, (slot == 1) != other_sender))
        if kind == "half":
            blocks.append((ref, 0))
            frames.append(block_frame(place, distance, other_sender))
    fill_bias(bias_ref, frames, counts_ref, plane, core)
    rows = lax.broadcasted_iota(jnp.int32, (FRAME, 128), 1)
    for j in range(COLUMNS):
        hot_ref[j * FRAME : (j + 1) * FRAME, :] = jnp.where(rows == j, 1.0, 0.0).astype(jnp.bfloat16)
    keys_n = len(blocks) * FRAME
    ones = jnp.ones((keys_n, 128), jnp.bfloat16)
    lanes = lax.broadcasted_iota(jnp.int32, (Q_TILE, 128), 1)
    for t in range(COLUMNS * FRAME // Q_TILE):
        at = slice(t * Q_TILE, (t + 1) * Q_TILE)
        frames_at = slice(t * Q_TILE // FRAME, (t + 1) * Q_TILE // FRAME)
        tops = jnp.zeros((Q_TILE, 128), jnp.float32)
        totals = jnp.zeros((Q_TILE, 128), jnp.float32)
        for h in range(HEADS):
            cols = slice(h * HEAD_DIM, (h + 1) * HEAD_DIM)
            k_head = jnp.concatenate([ref[slot, 0, :, cols] for ref, slot in blocks], axis=0)
            v_head = jnp.concatenate([ref[slot, 1, :, cols] for ref, slot in blocks], axis=0)
            k_wide = jnp.concatenate([k_head, bias_ref[...]], axis=1)
            v_wide = jnp.concatenate([v_head, ones], axis=1)
            q_head = q_ref[frames_at, :, cols].reshape(Q_TILE, HEAD_DIM)
            q_wide = jnp.concatenate([q_head, hot_ref[at, :]], axis=1)
            scores = lax.dot_general(
                q_wide, k_wide, (((1,), (1,)), ((), ())), preferred_element_type=jnp.float32
            )
            top = jnp.broadcast_to(jnp.max(scores, axis=1, keepdims=True), (Q_TILE, 128))
            if has_state:
                before = max_in[h, at, :]
                top = jnp.maximum(top, before)
            else:
                top = jnp.maximum(top, FLOOR)
            weights = jnp.exp2((scores - jnp.tile(top, (1, keys_n // 128))) * EXP2_SCALE).astype(
                jnp.bfloat16
            )
            both = jnp.dot(weights, v_wide, preferred_element_type=jnp.float32)
            acc, total = both[:, :HEAD_DIM], both[:, HEAD_DIM:]
            if has_state:
                fade = jnp.exp2((before - top) * EXP2_SCALE)
                acc = acc + acc_in[at, cols] * fade
                total = total + sum_in[h, at, :] * fade
            if not last:
                outs[0][at, cols] = acc
                outs[1][h, at, :] = top
                outs[2][h, at, :] = total
            else:
                tops = jnp.where(lanes == h, top, tops)
                totals = jnp.where(lanes == h, total, totals)
                mean = (acc * (1.0 / jnp.maximum(total, 1e-30))).astype(jnp.bfloat16)
                head_rows = slice(h * FRAME, (h + 1) * FRAME)
                outs[0][frames_at, head_rows, :] = mean.reshape(Q_TILE // FRAME, FRAME, HEAD_DIM)
        if last:
            packed, slot = jnp.zeros((Q_TILE, 128), jnp.float32), 0
            for value, count in ((tops, TOP_PARTS), (totals, TOTAL_PARTS)):
                for _ in range(count):
                    part = value.astype(jnp.bfloat16).astype(jnp.float32)
                    value = value - part
                    packed = packed + (pltpu.roll(part, slot * HEADS, 1) if slot else part)
                    slot += 1
            packed = packed.reshape(Q_TILE // FRAME, FRAME, 128)
            for i in range(Q_TILE // FRAME):
                folded = packed[i, :STATS]
                for k in range(1, FRAME // STATS):
                    folded = folded + pltpu.roll(packed[i, k * STATS : (k + 1) * STATS], 32 * k, 1)
                outs[0][t * (Q_TILE // FRAME) + i, HEADS * FRAME :, :] = folded.astype(jnp.bfloat16)


def attend_call(place, counts, q_all, kv, offsets, state, last):
    rows = COLUMNS * FRAME
    keys_n = sum(1 if kind == "half" else 2 for kind, _, _ in offsets) * FRAME
    if last:
        out_shape = jax.ShapeDtypeStruct((COLUMNS, SENT_ROWS, HEAD_DIM), jnp.bfloat16)
        out_specs = pl.BlockSpec(memory_space=pltpu.VMEM)
    else:
        out_shape = [
            jax.ShapeDtypeStruct((rows, WIDE), jnp.float32),
            jax.ShapeDtypeStruct((HEADS, rows, 128), jnp.float32),
            jax.ShapeDtypeStruct((HEADS, rows, 128), jnp.float32),
        ]
        out_specs = [pl.BlockSpec(memory_space=pltpu.VMEM)] * 3
    vmem = pl.BlockSpec(memory_space=pltpu.VMEM)
    smem = pl.BlockSpec(memory_space=pltpu.SMEM)
    flops = 2 * 2 * rows * keys_n * WIDE
    return pl.pallas_call(
        functools.partial(attend, offsets, state is not None, last),
        out_shape=out_shape,
        in_specs=[smem, smem] + [vmem] * (1 + len(kv) + (3 if state is not None else 0)),
        out_specs=out_specs,
        scratch_shapes=[
            pltpu.VMEM((keys_n, 128), jnp.bfloat16),
            pltpu.VMEM((rows, 128), jnp.bfloat16),
        ],
        compiler_params=pltpu.CompilerParams(vmem_limit_bytes=24 * 2**20),
        cost_estimate=pl.CostEstimate(
            flops=flops, bytes_accessed=4 * 2**20, transcendentals=rows * keys_n * HEADS
        ),
        name="attend_last" if last else "attend_first",
    )(place, counts, q_all, *kv, *(state if state is not None else ()))


def project(own, place_ref, counts_ref, parts_ref, wo_ref, out_ref, share_ref):
    plane, column, core, tp = place_ref[0], place_ref[1], place_ref[2], place_ref[3]
    frame = (plane * COLUMNS + column) * 2 + core
    rows = lax.broadcasted_iota(jnp.int32, (FRAME, 1), 0)
    live = rows < counts_ref[frame]

    def part(stats, i):
        return pltpu.roll(stats, 128 - HEADS * i, 1) if i else stats

    tops, totals = [], []
    for j in range(COLUMNS):
        folded = parts_ref[j, HEADS * FRAME :, :].astype(jnp.float32)
        stats = jnp.concatenate(
            [folded] + [pltpu.roll(folded, 128 - 32 * k, 1) for k in range(1, FRAME // STATS)], axis=0
        )
        tops.append(sum(part(stats, i) for i in range(1, TOP_PARTS)) + stats)
        totals.append(sum(part(stats, TOP_PARTS + i) for i in range(TOTAL_PARTS)))
    top = functools.reduce(jnp.maximum, tops)
    shares = [n * jnp.exp2((m - top) * EXP2_SCALE) for m, n in zip(tops, totals)]
    total = functools.reduce(jnp.add, shares)
    for j, share in enumerate(shares):
        share_ref[j] = jnp.where(live, share / total, 0.0)
    half = FRAME // 2
    first = (tp if own else 1 - tp) * half
    heads = []
    for h in range(HEADS):
        at = pl.ds(pl.multiple_of(h * FRAME + first, half), half)
        share_at = pl.ds(pl.multiple_of(first, half), half)
        heads.append(
            functools.reduce(
                jnp.add,
                [
                    parts_ref[j, at, :].astype(jnp.float32) * share_ref[j, share_at, h : h + 1]
                    for j in range(COLUMNS)
                ],
            ).astype(jnp.bfloat16)
        )
    att = jnp.concatenate(heads, axis=1)
    step = 512
    for n in range(0, wo_ref.shape[1], step):
        out_ref[:, n : n + step] = jnp.dot(
            att, wo_ref[:, n : n + step], preferred_element_type=jnp.float32
        ).astype(out_ref.dtype)


def project_call(place, counts, parts, wo, own):
    vmem = pl.BlockSpec(memory_space=pltpu.VMEM)
    smem = pl.BlockSpec(memory_space=pltpu.SMEM)
    return pl.pallas_call(
        functools.partial(project, own),
        out_shape=jax.ShapeDtypeStruct(
            (FRAME // 2, wo.shape[1]), jnp.float32 if own else jnp.bfloat16
        ),
        in_specs=[smem, smem, vmem, vmem],
        out_specs=vmem,
        scratch_shapes=[pltpu.VMEM((COLUMNS, FRAME, 128), jnp.float32)],
        compiler_params=pltpu.CompilerParams(vmem_limit_bytes=24 * 2**20),
        name="project_own" if own else "project_partner",
    )(place, counts, parts, wo)


SWAP = [(0, 1), (1, 0)]


def split_ring(distance):
    return [
        (z * 2 + c, (z + (distance if c == 0 else -distance)) % PLANES * 2 + c)
        for z in range(PLANES)
        for c in range(2)
    ]


def on_device(queries, keys, values, wo, frame_tokens):
    place = jnp.stack(
        [
            lax.axis_index("z"),
            lax.axis_index("xh") * 4 + lax.axis_index("y"),
            lax.axis_index("core"),
            lax.axis_index("tp"),
        ]
    ).astype(jnp.int32)
    own = jnp.stack([keys, values])
    own2 = jnp.stack([own, lax.ppermute(own, "core", SWAP)])
    zc = ("z", "core")
    queries, own2 = lax.optimization_barrier((queries, own2))
    second = lax.ppermute(own2, zc, split_ring(2))
    near = lax.ppermute(own2, zc, split_ring(1))
    q_all = lax.all_to_all(
        jnp.broadcast_to(queries[None], (COLUMNS, FRAME, WIDE)), ("xh", "y"), 0, 0, tiled=True
    )
    fourth = lax.ppermute(second[:1], zc, split_ring(2))
    third = lax.ppermute(second, zc, split_ring(1))
    near, q_all = lax.optimization_barrier((near, q_all))
    second_o = lax.ppermute(second, "core", SWAP)
    state = attend_call(
        place,
        frame_tokens,
        q_all,
        [own2, near, second, second_o],
        [("both", 0, False), ("both", 1, False), ("both", 2, False), ("both", 2, True)],
        None,
        False,
    )
    near_o = lax.ppermute(near, "core", SWAP)
    third, fourth, state = lax.optimization_barrier((third, fourth, state))
    third_o = lax.ppermute(third, "core", SWAP)
    fourth_o = lax.ppermute(fourth, "core", SWAP)
    rest = [near_o, third, third_o, fourth, fourth_o]
    rest_off = [
        ("both", 1, True),
        ("both", 3, False),
        ("both", 3, True),
        ("half", 4, False),
        ("half", 4, True),
    ]
    partial = attend_call(place, frame_tokens, q_all, rest, rest_off, state, True)
    parts = lax.all_to_all(partial, ("xh", "y"), 0, 0, tiled=True)
    got = lax.ppermute(project_call(place, frame_tokens, parts, wo, False), "tp", SWAP)
    keep = project_call(place, frame_tokens, parts, wo, True)
    return (keep + got.astype(jnp.float32)).astype(jnp.bfloat16)


def solution(mesh):
    fine = Mesh(mesh.devices.reshape(PLANES, 2, 4, 2, 2), CTX + ("tp",))
    in_specs = (P(CTX, "tp"), P(CTX, "tp"), P(CTX, "tp"), P("tp", None), P())
    out_specs = P(CTX + ("tp",), None)
    return jax.shard_map(
        on_device, mesh=fine, in_specs=in_specs, out_specs=out_specs, check_vma=False
    )
```
